32 devices in a mesh: dp: 4 (over z), row: 4 (over x, core), col: 2 (over y).
Axes of the slice: x: 2, y: 2, z: 4, core: 2. Of those that a mesh axis runs over, the one named last changes fastest.
Arguments:
- tokens: bfloat16 [32768, 1024], P(('dp', 'row'), 'col'), may hold values from -6 to 6
- segment_ids: int32 [32768], P('dp'), may hold values from 0 to 3, as said below
- norm_one: float32 [1024], P('col'), may hold values from 0.3 to 4.6
- qkv_weight: bfloat16 [1024, 3, 16, 64], P('col', None, 'row'), may hold values from -0.1875 to 0.1875
- attn_out_weight: bfloat16 [1024, 1024], P('row', 'col'), may hold values from -0.75 to 0.75
- norm_two: float32 [1024], P('col'), may hold values from 0.3 to 4.6
- in_weight: bfloat16 [1024, 2, 2624], P('col', None, 'row'), may hold values from -0.1875 to 0.1875
- out_weight: bfloat16 [2624, 1024], P('row', 'col'), may hold values from -0.125 to 0.125
- cotangent: bfloat16 [32768, 1024], P(('dp', 'row'), 'col'), may hold values from -6 to 6
Outputs:
- result: bfloat16 [32768, 1024], P(('dp', 'row'), 'col')
- grad_tokens: float32 [32768, 1024], P(('dp', 'row'), 'col')
- grad_norm_one: float32 [1024], P('col')
- grad_qkv: float32 [1024, 3, 16, 64], P('col', None, 'row')
- grad_attn_out: float32 [1024, 1024], P('row', 'col')
- grad_norm_two: float32 [1024], P('col')
- grad_in: float32 [1024, 2, 2624], P('col', None, 'row')
- grad_out: float32 [2624, 1024], P('row', 'col')
The draws below stay inside these ranges and needn't reach their ends.
Inputs may be any that keep to these rules, and one draw needn't show every extreme that they name: `segment_ids`: each sequence of 4096 tokens (aligned blocks of the array) holds 4 documents numbered from 0 in order, each of 200 tokens or more, one of exactly 2000 tokens.
All inputs are finite; a program needn't handle non-finite values.
Results may differ from the reference program's by a relative error of at most 0.018.
Values may be sent and summed in bfloat16 or wider, within the bound.
A program may use at most 256 MiB of HBM per device.

```python
import jax
import jax.numpy as jnp
from jax import lax

D = 1024
H = 16
HD = 64
FF = 2624
WINDOW = 128
SEQ = 4096
DOCS = 4
DOC_MOST = 2000
DOC_LEAST = 200
TOKENS = 32768


def document_ids(key):
    cut_key = jax.random.fold_in(key, 11)
    place_key = jax.random.fold_in(key, 12)
    spare = SEQ - DOC_MOST - 3 * DOC_LEAST
    cut_points = jax.random.randint(cut_key, (2,), 0, spare + 1)
    lower_cut = jnp.minimum(cut_points[0], cut_points[1])
    upper_cut = jnp.maximum(cut_points[0], cut_points[1])
    others = jnp.stack([lower_cut, upper_cut - lower_cut, spare - upper_cut]) + DOC_LEAST
    longest = jax.random.randint(place_key, (), 0, DOCS)
    places = jnp.arange(DOCS, dtype=jnp.int32)
    source = jnp.clip(places - (places > longest).astype(jnp.int32), 0, DOCS - 2)
    lengths = jnp.where(places == longest, DOC_MOST, others[source])
    bounds = jnp.cumsum(lengths)
    positions = jnp.arange(SEQ, dtype=jnp.int32)
    return jnp.sum((positions[:, None] >= bounds[None, :DOCS - 1]).astype(jnp.int32), axis=1)


def draw_segment_ids(key, part):
    key = jax.random.fold_in(key, 5)
    seq_keys = jax.random.split(key, TOKENS // SEQ)
    return jax.vmap(document_ids)(seq_keys).reshape(TOKENS).astype(jnp.int32)


def rising_gain(key, start, ratio, jitter):
    place = jnp.arange(D, dtype=jnp.float32) / (D - 1)
    noise = jax.random.uniform(key, (D,), jnp.float32, 1.0 - jitter, 1.0 + jitter)
    return (start * ratio ** place * noise).astype(jnp.float32)


def draw_norm_one(key, part):
    key = jax.random.fold_in(key, 21)
    return rising_gain(key, 0.6, 5.0, 0.15)


def draw_norm_two(key, part):
    key = jax.random.fold_in(key, 22)
    return rising_gain(key, 0.6, 5.0, 0.15)


def steps_of(stream_key, shape, pieces, low, largest):
    level = 1.0
    for position, blocks in pieces:
        draws = jax.random.uniform(jax.random.fold_in(jax.random.fold_in(stream_key, 6), position), (blocks,), jnp.float32, low / len(pieces), largest / len(pieces))
        level = level * jnp.repeat(jnp.exp(draws), shape[position] // blocks).reshape((-1,) + (1,) * (len(shape) - 1 - position))
    return level


def normal_values(own_key, dims, spread, reach, pieces=(), kind=jnp.bfloat16):
    loudness = steps_of(own_key, dims, pieces, -0.22, 0.18) if pieces else 1.0
    array = jax.random.normal(own_key, dims, jnp.float32) * spread * loudness
    return jnp.minimum(jnp.maximum(array, -reach), reach).astype(kind)


def setup_inputs(seed: int = 0) -> dict:
    key_list = jax.random.split(jax.random.key(seed), 10)
    tokens = normal_values(key_list[0], (TOKENS, D), 1.0, 6.0, ((0, 16), (1, 2)))
    segment_ids = draw_segment_ids(jax.random.fold_in(key_list[9], 71), 0)
    norm_one = draw_norm_one(jax.random.fold_in(key_list[9], 71), 0)
    qkv_weight = normal_values(key_list[3], (D, 3, H, HD), D ** -0.5, 0.1875, ((0, 2), (2, 4)))
    attn_out_weight = normal_values(key_list[4], (D, D), (D // 16) ** -0.5, 0.75, ((0, 4), (1, 2)))
    norm_two = draw_norm_two(jax.random.fold_in(key_list[9], 71), 0)
    in_weight = normal_values(key_list[6], (D, 2, FF), D ** -0.5, 0.1875, ((0, 2), (2, 4)))
    out_weight = normal_values(key_list[7], (FF, D), FF ** -0.5, 0.125, ((0, 4), (1, 2)))
    cotangent = normal_values(key_list[8], (TOKENS, D), 1.0, 6.0, ((0, 16), (1, 2)))
    return dict(tokens=tokens, segment_ids=segment_ids, norm_one=norm_one, qkv_weight=qkv_weight, attn_out_weight=attn_out_weight, norm_two=norm_two, in_weight=in_weight, out_weight=out_weight, cotangent=cotangent)


EPS = 1e-05
NEG = -1e+30
THETA = 10000.0
HIGH = lax.Precision.HIGHEST

@jax.custom_vjp
def low(v):
    return lax.optimization_barrier(v.astype(jnp.bfloat16)).astype(jnp.float32)

@jax.custom_vjp
def low_back(v):
    return v

def low_keep(v):
    return (low(v), None)

def low_pass(kept, grad):
    return (grad,)

def back_keep(v):
    return (v, None)

def back_low(kept, grad):
    return (low(grad),)
low.defvjp(low_keep, low_pass)
low_back.defvjp(back_keep, back_low)

def layer_norm(inputs, gain_vec):
    average = lax.optimization_barrier(jnp.mean(inputs, -1, keepdims=True))
    centred = inputs - average
    variance = lax.optimization_barrier(jnp.mean(centred * centred, -1, keepdims=True))
    return centred * lax.rsqrt(variance + EPS) * gain_vec

def rotary_tables(length, head_size):
    frequencies = THETA ** (-jnp.arange(head_size // 2, dtype=jnp.float32) * 2.0 / head_size)
    angles = jnp.arange(length, dtype=jnp.float32)[:, None] * frequencies[None, :]
    angles = jnp.concatenate([angles, angles], -1)
    return (jnp.cos(angles), jnp.sin(angles))

def rotate(values_in, cos_tab, sin_tab):
    half_size = values_in.shape[-1] // 2
    turned = jnp.concatenate([-values_in[..., half_size:], values_in[..., :half_size]], -1)
    return values_in * cos_tab[:, None, :] + turned * sin_tab[:, None, :]

def attend(queries, key_vecs, values, segments):
    half_win = WINDOW // 2
    block_len = min(512, SEQ)
    key_span = block_len + 2 * half_win
    pad_spec = ((half_win, half_win), (0, 0), (0, 0))
    key_pad = jnp.pad(key_vecs, pad_spec)
    value_pad = jnp.pad(values, pad_spec)
    seg_pad = jnp.pad(segments, (half_win, half_win), constant_values=-1)
    scaling = HD ** (-0.5)

    def one_block(offset):
        query_blk = lax.dynamic_slice_in_dim(queries, offset, block_len, 0)
        key_blk = lax.dynamic_slice_in_dim(key_pad, offset, key_span, 0)
        value_blk = lax.dynamic_slice_in_dim(value_pad, offset, key_span, 0)
        seg_query = lax.dynamic_slice_in_dim(seg_pad, offset + half_win, block_len, 0)
        seg_key = lax.dynamic_slice_in_dim(seg_pad, offset, key_span, 0)
        distance = jnp.arange(key_span, dtype=jnp.int32)[None, :] - jnp.arange(block_len, dtype=jnp.int32)[:, None] - half_win
        allowed = (seg_query[:, None] == seg_key[None, :]) & (jnp.abs(distance) <= half_win)
        scores = jnp.einsum('qhd,khd->hqk', query_blk, key_blk, precision=HIGH) * scaling
        scores = low_back(jnp.where(allowed[None], scores, NEG))
        highest = lax.optimization_barrier(jnp.max(scores, -1, keepdims=True))
        weights = jnp.exp(scores - highest)
        attn_probs = low(weights / lax.optimization_barrier(jnp.sum(weights, -1, keepdims=True)))
        return jnp.einsum('hqk,khd->qhd', attn_probs, value_blk, precision=HIGH)
    offsets = jnp.arange(SEQ // block_len, dtype=jnp.int32) * block_len
    mixture = lax.map(jax.checkpoint(one_block), offsets)
    return mixture.reshape(SEQ, H, HD)

def layer_forward(inputs, segments, norm_one, qkv_weight, attn_out_weight, norm_two, in_weight, out_weight):
    normed = low(layer_norm(inputs, norm_one))
    joined = low_back(jnp.dot(normed, qkv_weight.reshape(D, 3 * D), precision=HIGH)).reshape(SEQ, 3, H, HD)
    cos_tab, sin_tab = rotary_tables(SEQ, HD)
    queries = low(rotate(joined[:, 0], cos_tab, sin_tab))
    key_vecs = low(rotate(joined[:, 1], cos_tab, sin_tab))
    values = low(joined[:, 2])
    mixture = low_back(low(attend(queries, key_vecs, values, segments))).reshape(SEQ, D)
    hidden = inputs + low_back(jnp.dot(mixture, attn_out_weight, precision=HIGH))
    normed_two = low(layer_norm(hidden, norm_two))
    before = low_back(jnp.dot(normed_two, in_weight.reshape(D, 2 * FF), precision=HIGH)).reshape(SEQ, 2, FF)
    active = low(jax.nn.gelu(before[:, 0], approximate=False) * before[:, 1])
    return hidden + low_back(jnp.dot(active, out_weight, precision=HIGH))

def reference(tokens, segment_ids, norm_one, qkv_weight, attn_out_weight, norm_two, in_weight, out_weight, cotangent):
    seq_count = TOKENS // SEQ
    inputs = tokens.astype(jnp.float32).reshape(seq_count, SEQ, D)
    cotangents = cotangent.astype(jnp.float32).reshape(seq_count, SEQ, D)
    segments = segment_ids.reshape(seq_count, SEQ)
    params = (norm_one.astype(jnp.float32), qkv_weight.astype(jnp.float32), attn_out_weight.astype(jnp.float32), norm_two.astype(jnp.float32), in_weight.astype(jnp.float32), out_weight.astype(jnp.float32))

    def one_sequence(totals, scan_item):
        seq_inputs, seq_segments, seq_cotangent = scan_item

        def forward(layer_in, *weights):
            return layer_forward(layer_in, seq_segments, *weights)
        output, pullback = jax.vjp(forward, seq_inputs, *params)
        grads = pullback(seq_cotangent)
        totals = tuple((total_one + grad_one for total_one, grad_one in zip(totals, grads[1:])))
        return (totals, (output.astype(jnp.bfloat16), grads[0]))
    zeros_init = tuple((jnp.zeros_like(param_one) for param_one in params))
    totals, (outputs, input_grads) = lax.scan(one_sequence, zeros_init, (inputs, segments, cotangents))
    return (outputs.reshape(TOKENS, D), input_grads.reshape(TOKENS, D), totals[0], totals[1], totals[2], totals[3], totals[4], totals[5])
```

```python
import functools

import jax
import jax.numpy as jnp
from jax import lax
from jax.experimental import pallas as pl
from jax.experimental.pallas import tpu as pltpu
from jax.sharding import PartitionSpec as P

WINDOW = 128
HALF = WINDOW // 2
SEQ = 4096
BLOCK = 128
PAIR = 128

EPS = 1e-05
NEG = -1e30
THETA = 10000.0
PLANE = ("row", "col")
VMEM_LIMIT = 48 * 1024 * 1024


def dot_nn(left, right):
    return jnp.dot(left, right, preferred_element_type=jnp.float32)


def dot_nt(left, right):
    return lax.dot_general(
        left, right, (((1,), (1,)), ((), ())), preferred_element_type=jnp.float32
    )


def dot_tn(left, right):
    return lax.dot_general(
        left, right, (((0,), (0,)), ((), ())), preferred_element_type=jnp.float32
    )


def first_half(shape):
    return lax.broadcasted_iota(jnp.int32, shape, 1) % 64 < 32


def turn(values_in):
    ahead = pltpu.roll(values_in, PAIR - 32, 1)
    behind = pltpu.roll(values_in, 32, 1)
    return jnp.where(first_half(values_in.shape), -ahead, behind)


def turn_back(values_in):
    ahead = pltpu.roll(values_in, PAIR - 32, 1)
    behind = pltpu.roll(values_in, 32, 1)
    return jnp.where(first_half(values_in.shape), ahead, -behind)


def forward_kernel(
    blocks, normed_ref, wq_ref, wk_ref, wv_ref, cos_ref, sin_ref, bias_ref, q_ref, k_ref, v_ref, mix_ref
):
    cos_tab = cos_ref[...]
    sin_tab = sin_ref[...]
    own = pl.ds(HALF, blocks * BLOCK)
    queries = dot_nn(normed_ref[own, :], wq_ref[...])
    queries = queries * cos_tab[HALF:-HALF] + turn(queries) * sin_tab[HALF:-HALF]
    q_ref[...] = queries.astype(jnp.bfloat16) * jnp.bfloat16(0.125)
    keys = dot_nn(normed_ref[...], wk_ref[...])
    keys = keys * cos_tab + turn(keys) * sin_tab
    k_ref[...] = keys.astype(jnp.bfloat16)
    v_ref[...] = dot_nn(normed_ref[...], wv_ref[...]).astype(jnp.bfloat16)
    lower = lax.broadcasted_iota(jnp.int32, (BLOCK, PAIR), 1) < 64
    for block in range(blocks):
        rows = pl.ds(block * BLOCK, BLOCK)
        span = pl.ds(block * BLOCK, BLOCK + WINDOW)
        q_blk = q_ref[rows, :]
        k_blk = k_ref[span, :]
        v_blk = v_ref[span, :]
        bias = bias_ref[rows, :]
        outs = []
        for head in range(2):
            q_head = jnp.where(lower if head == 0 else ~lower, q_blk, jnp.bfloat16(0))
            scores = dot_nt(q_head, k_blk) + bias
            weights = jnp.exp(scores - jnp.max(scores, -1, keepdims=True))
            probs = weights * (1.0 / jnp.sum(weights, -1, keepdims=True))
            outs.append(dot_nn(probs.astype(jnp.bfloat16), v_blk))
        mix_ref[rows, :] = jnp.where(lower, outs[0], outs[1]).astype(jnp.bfloat16)


def backward_kernel(
    blocks, q_ref, k_ref, v_ref, grad_ref, cos_ref, sin_ref, bias_ref, dq_ref, dk_ref, dv_ref, dk_acc, dv_acc
):
    dk_acc[...] = jnp.zeros_like(dk_acc)
    dv_acc[...] = jnp.zeros_like(dv_acc)
    lower = lax.broadcasted_iota(jnp.int32, (BLOCK, PAIR), 1) < 64
    for block in range(blocks):
        rows = pl.ds(block * BLOCK, BLOCK)
        span = pl.ds(block * BLOCK, BLOCK + WINDOW)
        own = pl.ds(block * BLOCK + HALF, BLOCK)
        q_blk = q_ref[rows, :]
        k_blk = k_ref[span, :]
        v_blk = v_ref[span, :]
        g_blk = grad_ref[rows, :]
        bias = bias_ref[rows, :]
        dq_parts = []
        dk_part = 0.0
        dv_part = 0.0
        for head in range(2):
            mask = lower if head == 0 else ~lower
            q_head = jnp.where(mask, q_blk, jnp.bfloat16(0))
            g_head = jnp.where(mask, g_blk, jnp.bfloat16(0))
            scores = dot_nt(q_head, k_blk) + bias
            weights = jnp.exp(scores - jnp.max(scores, -1, keepdims=True))
            probs = weights * (1.0 / jnp.sum(weights, -1, keepdims=True))
            grad_probs = dot_nt(g_head, v_blk)
            centre = jnp.sum(grad_probs * probs, -1, keepdims=True)
            grad_scores = (probs * (grad_probs - centre)).astype(jnp.bfloat16)
            dq_parts.append(dot_nn(grad_scores, k_blk))
            dk_part += dot_tn(grad_scores, q_head)
            dv_part += dot_tn(probs.astype(jnp.bfloat16), g_head)
        dk_acc[span, :] += dk_part
        dv_acc[span, :] += dv_part
        dq = jnp.where(lower, dq_parts[0], dq_parts[1]) * 0.125
        dq = dq * cos_ref[own, :] + turn_back(dq * sin_ref[own, :])
        dq_ref[rows, :] = dq.astype(jnp.bfloat16)
    dk = dk_acc[...]
    dk_ref[...] = (dk * cos_ref[...] + turn_back(dk * sin_ref[...])).astype(jnp.bfloat16)
    dv_ref[...] = dv_acc[...].astype(jnp.bfloat16)


def column_block(rows, first=0):
    return pl.BlockSpec((rows, PAIR), lambda pair: (0, first + pair))


def whole_block(shape):
    return pl.BlockSpec(shape, lambda pair: (0,) * len(shape))


def attend(normed_ext, qkv_full, cos_tab, sin_tab, bias):
    ext, width = normed_ext.shape
    count = ext - 2 * HALF
    pairs = width // PAIR
    kind = jnp.bfloat16
    return pl.pallas_call(
        functools.partial(forward_kernel, count // BLOCK),
        grid=(pairs,),
        in_specs=[
            whole_block(normed_ext.shape),
            column_block(width),
            column_block(width, pairs),
            column_block(width, 2 * pairs),
            whole_block(cos_tab.shape),
            whole_block(sin_tab.shape),
            whole_block(bias.shape),
        ],
        out_specs=[column_block(count), column_block(ext), column_block(ext), column_block(count)],
        out_shape=[
            jax.ShapeDtypeStruct((count, width), kind),
            jax.ShapeDtypeStruct((ext, width), kind),
            jax.ShapeDtypeStruct((ext, width), kind),
            jax.ShapeDtypeStruct((count, width), kind),
        ],
        compiler_params=pltpu.CompilerParams(vmem_limit_bytes=VMEM_LIMIT),
        cost_estimate=pl.CostEstimate(
            flops=2 * ext * width * 3 * width + 4 * count * 256 * 128 * 16,
            bytes_accessed=2 * (3 * width * width + 5 * ext * width),
            transcendentals=count * 256 * 16,
        ),
        name="attend_forward",
    )(normed_ext, qkv_full, qkv_full, qkv_full, cos_tab, sin_tab, bias)


def attend_back(queries, keys, values, grad_mixture, cos_tab, sin_tab, bias):
    ext, width = keys.shape
    count = ext - 2 * HALF
    kind = jnp.bfloat16
    return pl.pallas_call(
        functools.partial(backward_kernel, count // BLOCK),
        grid=(width // PAIR,),
        in_specs=[
            column_block(count),
            column_block(ext),
            column_block(ext),
            column_block(count),
            whole_block(cos_tab.shape),
            whole_block(sin_tab.shape),
            whole_block(bias.shape),
        ],
        out_specs=[column_block(count), column_block(ext), column_block(ext)],
        out_shape=[
            jax.ShapeDtypeStruct((count, width), kind),
            jax.ShapeDtypeStruct((ext, width), kind),
            jax.ShapeDtypeStruct((ext, width), kind),
        ],
        scratch_shapes=[pltpu.VMEM((ext, PAIR), jnp.float32), pltpu.VMEM((ext, PAIR), jnp.float32)],
        compiler_params=pltpu.CompilerParams(vmem_limit_bytes=VMEM_LIMIT),
        cost_estimate=pl.CostEstimate(
            flops=12 * count * 256 * 128 * 16,
            bytes_accessed=2 * 7 * ext * width,
            transcendentals=count * 256 * 16,
        ),
        name="attend_backward",
    )(queries, keys, values, grad_mixture, cos_tab, sin_tab, bias)


def unit_rows(inputs):
    average = jnp.mean(inputs, 1, keepdims=True)
    centred = inputs - average
    inverse_std = lax.rsqrt(jnp.mean(centred * centred, 1, keepdims=True) + EPS)
    return centred * inverse_std, inverse_std


def norm_backward(grad_normed, unit, inverse_std, gain_vec):
    scaled = grad_normed * gain_vec
    average = jnp.mean(scaled, 1, keepdims=True)
    cross = jnp.mean(scaled * unit, 1, keepdims=True)
    return inverse_std * (scaled - average - unit * cross), jnp.sum(grad_normed * unit, 0)


def whole_rows(array_in):
    return lax.all_to_all(array_in, "col", 0, 1, tiled=True)


def split_rows(array_in):
    return lax.all_to_all(array_in, "col", 1, 0, tiled=True)


def gather_plane(local):
    return lax.all_gather(local, PLANE, axis=0, tiled=False)


def sum_plane(stacked):
    part = lax.psum_scatter(stacked, PLANE, scatter_dimension=0, tiled=False)
    return lax.psum(part, "dp").astype(jnp.float32)


def gelu_parts(pre):
    cdf = 0.5 * (1.0 + lax.erf(pre * 0.7071067811865476))
    slope = cdf + pre * jnp.exp(-0.5 * pre * pre) * 0.3989422804014327
    return pre * cdf, slope


def shards(
    tokens,
    segment_ids,
    norm_one,
    qkv_weight,
    attn_out_weight,
    norm_two,
    in_weight,
    out_weight,
    cotangent,
):
    rows, cols = lax.axis_size("row"), lax.axis_size("col")
    plane = rows * cols
    place = lax.axis_index("row") * cols + lax.axis_index("col")
    feat = tokens.shape[1]
    width = feat * cols
    heads_width = qkv_weight.shape[2] * qkv_weight.shape[3]
    hidden = in_weight.shape[2]
    low = jnp.bfloat16

    qkv_stack = gather_plane(qkv_weight.reshape(feat, 3, heads_width))
    qkv_full = qkv_stack.reshape(rows, cols, feat, 3, heads_width)
    qkv_full = qkv_full.transpose(1, 2, 3, 0, 4).reshape(width, 3 * width)

    def out_full(local):
        stack = gather_plane(local)
        stack = stack.reshape((rows, cols) + local.shape).transpose(0, 2, 1, 3)
        return stack.reshape(rows * local.shape[0], width)

    attn_full = out_full(attn_out_weight)
    in_stack = gather_plane(in_weight.transpose(1, 2, 0))
    in_full = in_stack.reshape(rows, cols, 2, hidden, feat).transpose(2, 0, 3, 1, 4)
    in_full = in_full.reshape(2, rows * hidden, width)
    ffn_out_full = out_full(out_weight)
    gain_one, gain_two = lax.all_gather(jnp.stack([norm_one, norm_two]), "col", axis=1, tiled=True)

    own_tokens = whole_rows(tokens)
    own_cotangent = whole_rows(cotangent)
    count = own_tokens.shape[0]
    ahead = [(i, i + 1) for i in range(plane - 1)]
    behind = [(i + 1, i) for i in range(plane - 1)]
    before_rows = lax.ppermute(own_tokens[-HALF:], PLANE, ahead)
    after_rows = lax.ppermute(own_tokens[:HALF], PLANE, behind)
    residual_ext = jnp.concatenate([before_rows, own_tokens, after_rows], 0).astype(jnp.float32)
    unit_ext, inverse_ext = unit_rows(residual_ext)
    normed_ext = (unit_ext * gain_one).astype(low)
    normed_one = normed_ext[HALF:-HALF]

    total = segment_ids.shape[0]
    marks = segment_ids + 16 * (lax.iota(jnp.int32, total) // SEQ)
    marks = jnp.pad(marks, (HALF, HALF), constant_values=-1)
    marks = lax.dynamic_slice_in_dim(marks, place * count, count + 2 * HALF, 0)
    blocks = count // BLOCK
    key_marks = jnp.stack([marks[i * BLOCK : i * BLOCK + BLOCK + WINDOW] for i in range(blocks)])
    query_marks = marks[HALF:-HALF].reshape(blocks, BLOCK)
    shape = (BLOCK, BLOCK + WINDOW)
    distance = lax.broadcasted_iota(jnp.int32, shape, 1) - lax.broadcasted_iota(jnp.int32, shape, 0)
    near = jnp.abs(distance - HALF) <= HALF
    allowed = (query_marks[:, :, None] == key_marks[:, None, :]) & near[None]
    bias = jnp.where(allowed, 0.0, NEG).astype(jnp.float32).reshape(count, BLOCK + WINDOW)

    places = (place * count - HALF + lax.iota(jnp.int32, count + 2 * HALF)) % SEQ
    frequencies = THETA ** (-jnp.arange(32, dtype=jnp.float32) * 2.0 / 64)
    angles = places.astype(jnp.float32)[:, None] * frequencies[None, :]
    cos_tab = jnp.tile(jnp.cos(angles), (1, PAIR // 32))
    sin_tab = jnp.tile(jnp.sin(angles), (1, PAIR // 32))

    queries, keys, values, mixture = attend(normed_ext, qkv_full, cos_tab, sin_tab, bias)
    hidden_rows = own_tokens.astype(jnp.float32) + dot_nn(mixture, attn_full)
    unit_two, inverse_two = unit_rows(hidden_rows)
    normed_two = (unit_two * gain_two).astype(low)
    input_half = dot_nt(normed_two, in_full[0])
    gate_half = dot_nt(normed_two, in_full[1])
    grad_active = dot_nt(own_cotangent, ffn_out_full)
    gelu, slope = gelu_parts(input_half)
    active = (gelu * gate_half).astype(low)
    grad_input = (grad_active * gate_half * slope).astype(low)
    grad_gate = (grad_active * gelu).astype(low)
    active, grad_input, grad_gate = lax.optimization_barrier((active, grad_input, grad_gate))
    result = (hidden_rows + dot_nn(active, ffn_out_full)).astype(low)

    def out_stack(grad):
        grad = grad.reshape(rows, -1, cols, feat).transpose(0, 2, 1, 3)
        return grad.reshape(plane, -1, feat)

    grad_out = sum_plane(out_stack(dot_tn(active, own_cotangent).astype(low)))
    grad_in = jnp.stack([dot_tn(grad_input, normed_two), dot_tn(grad_gate, normed_two)]).astype(low)
    grad_in = grad_in.reshape(2, rows, hidden, cols, feat).transpose(1, 3, 0, 2, 4)
    grad_in = sum_plane(grad_in.reshape(plane, 2, hidden, feat)).transpose(2, 0, 1)
    grad_normed_two = dot_nn(grad_input, in_full[0]) + dot_nn(grad_gate, in_full[1])
    branch_two, sum_two = norm_backward(grad_normed_two, unit_two, inverse_two, gain_two)
    grad_hidden = own_cotangent.astype(jnp.float32) + branch_two
    grad_branch = grad_hidden.astype(low)

    grad_mixture = dot_nt(grad_branch, attn_full).astype(low)
    grad_attn = sum_plane(out_stack(dot_tn(mixture, grad_branch).astype(low)))
    dq, dk_ext, dv_ext = attend_back(queries, keys, values, grad_mixture, cos_tab, sin_tab, bias)
    edges = jnp.concatenate([dk_ext, dv_ext], 1)
    to_next = lax.ppermute(edges[-HALF:], PLANE, ahead)
    to_prev = lax.ppermute(edges[:HALF], PLANE, behind)
    middle = edges[HALF:-HALF]
    middle = jnp.concatenate(
        [
            (middle[:HALF].astype(jnp.float32) + to_next.astype(jnp.float32)).astype(low),
            middle[HALF:-HALF],
            (middle[-HALF:].astype(jnp.float32) + to_prev.astype(jnp.float32)).astype(low),
        ],
        0,
    )
    grad_joined = jnp.concatenate([dq, middle], 1)
    grad_qkv = dot_tn(normed_one, grad_joined).astype(low)
    grad_qkv = grad_qkv.reshape(cols, feat, 3, rows, heads_width).transpose(3, 0, 1, 2, 4)
    grad_qkv = sum_plane(grad_qkv.reshape(plane, feat, 3 * heads_width))
    grad_normed_one = dot_nt(grad_joined, qkv_full)
    branch_one, sum_one = norm_backward(
        grad_normed_one, unit_ext[HALF:-HALF], inverse_ext[HALF:-HALF], gain_one
    )
    grad_tokens = grad_hidden + branch_one

    sums = lax.psum(jnp.stack([sum_one, sum_two]), ("dp", "row", "col"))
    sums = lax.dynamic_slice_in_dim(sums, lax.axis_index("col") * feat, feat, 1)
    return (
        split_rows(result),
        split_rows(grad_tokens.astype(low)).astype(jnp.float32),
        sums[0],
        grad_qkv.reshape(qkv_weight.shape),
        grad_attn,
        sums[1],
        grad_in,
        grad_out,
    )


def solution(mesh):
    return jax.shard_map(
        shards,
        mesh=mesh,
        in_specs=(
            P(("dp", "row"), "col"),
            P("dp"),
            P("col"),
            P("col", None, "row", None),
            P("row", "col"),
            P("col"),
            P("col", None, "row"),
            P("row", "col"),
            P(("dp", "row"), "col"),
        ),
        out_specs=(
            P(("dp", "row"), "col"),
            P(("dp", "row"), "col"),
            P("col"),
            P("col", None, "row", None),
            P("row", "col"),
            P("col"),
            P("col", None, "row"),
            P("row", "col"),
        ),
        check_vma=False,
    )
```

```python
import functools

import jax
import jax.numpy as jnp
from jax import lax
from jax.experimental import pallas as pl
from jax.experimental.pallas import tpu as pltpu
from jax.sharding import PartitionSpec as P

WINDOW = 128
HALF = WINDOW // 2
SEQ = 4096
BLOCK = 128
PAIR = 128
LANES = 256

EPS = 1e-05
NEG = -1e30
THETA = 10000.0
PLANE = ("x", "core", "col")
CHIPS = ("x", "col")
VMEM_LIMIT = 48 * 1024 * 1024


def dot_nn(left, right):
    return jnp.dot(left, right, preferred_element_type=jnp.float32)


def dot_nt(left, right):
    return lax.dot_general(
        left, right, (((1,), (1,)), ((), ())), preferred_element_type=jnp.float32
    )


def dot_tn(left, right):
    return lax.dot_general(
        left, right, (((0,), (0,)), ((), ())), preferred_element_type=jnp.float32
    )


def first_half(shape):
    return lax.broadcasted_iota(jnp.int32, shape, 1) % 64 < 32


def turn(values_in):
    ahead = pltpu.roll(values_in, values_in.shape[1] - 32, 1)
    behind = pltpu.roll(values_in, 32, 1)
    return jnp.where(first_half(values_in.shape), -ahead, behind)


def turn_back(values_in):
    ahead = pltpu.roll(values_in, values_in.shape[1] - 32, 1)
    behind = pltpu.roll(values_in, 32, 1)
    return jnp.where(first_half(values_in.shape), ahead, -behind)


def forward_kernel(
    blocks, normed_ref, wq_ref, wk_ref, wv_ref, cos_ref, sin_ref, bias_ref, q_ref, k_ref, v_ref, mix_ref
):
    cos_tab = cos_ref[...]
    sin_tab = sin_ref[...]
    own = pl.ds(HALF, blocks * BLOCK)
    queries = dot_nt(normed_ref[own, :], wq_ref[0, 0])
    queries = queries * cos_tab[HALF:-HALF] + turn(queries) * sin_tab[HALF:-HALF]
    q_ref[...] = queries.astype(jnp.bfloat16) * jnp.bfloat16(0.125)
    keys = dot_nt(normed_ref[...], wk_ref[0, 0])
    keys = keys * cos_tab + turn(keys) * sin_tab
    k_ref[...] = keys.astype(jnp.bfloat16)
    v_ref[...] = dot_nt(normed_ref[...], wv_ref[0, 0]).astype(jnp.bfloat16)
    lower = lax.broadcasted_iota(jnp.int32, (BLOCK, PAIR), 1) < 64
    for block in range(blocks):
        rows = pl.ds(block * BLOCK, BLOCK)
        span = pl.ds(block * BLOCK, BLOCK + WINDOW)
        bias = bias_ref[rows, :]
        for pair in range(LANES // PAIR):
            lanes = pl.ds(pair * PAIR, PAIR)
            q_blk = q_ref[rows, lanes]
            k_blk = k_ref[span, lanes]
            v_blk = v_ref[span, lanes]
            outs = []
            for head in range(2):
                q_head = jnp.where(lower if head == 0 else ~lower, q_blk, jnp.bfloat16(0))
                scores = dot_nt(q_head, k_blk) + bias
                weights = jnp.exp(scores - jnp.max(scores, -1, keepdims=True))
                probs = weights * (1.0 / jnp.sum(weights, -1, keepdims=True))
                outs.append(dot_nn(probs.astype(jnp.bfloat16), v_blk))
            mix_ref[rows, lanes] = jnp.where(lower, outs[0], outs[1]).astype(jnp.bfloat16)


def backward_kernel(
    blocks, q_ref, k_ref, v_ref, grad_ref, cos_ref, sin_ref, bias_ref, dq_ref, dk_ref, dv_ref, dk_acc, dv_acc
):
    dk_acc[...] = jnp.zeros_like(dk_acc)
    dv_acc[...] = jnp.zeros_like(dv_acc)
    lower = lax.broadcasted_iota(jnp.int32, (BLOCK, PAIR), 1) < 64
    for block in range(blocks):
        rows = pl.ds(block * BLOCK, BLOCK)
        span = pl.ds(block * BLOCK, BLOCK + WINDOW)
        own = pl.ds(block * BLOCK + HALF, BLOCK)
        bias = bias_ref[rows, :]
        for pair in range(LANES // PAIR):
            lanes = pl.ds(pair * PAIR, PAIR)
            q_blk = q_ref[rows, lanes]
            k_blk = k_ref[span, lanes]
            v_blk = v_ref[span, lanes]
            g_blk = grad_ref[rows, lanes]
            dq_parts = []
            dk_part = 0.0
            dv_part = 0.0
            for head in range(2):
                mask = lower if head == 0 else ~lower
                q_head = jnp.where(mask, q_blk, jnp.bfloat16(0))
                g_head = jnp.where(mask, g_blk, jnp.bfloat16(0))
                scores = dot_nt(q_head, k_blk) + bias
                weights = jnp.exp(scores - jnp.max(scores, -1, keepdims=True))
                probs = weights * (1.0 / jnp.sum(weights, -1, keepdims=True))
                grad_probs = dot_nt(g_head, v_blk)
                centre = jnp.sum(grad_probs * probs, -1, keepdims=True)
                grad_scores = (probs * (grad_probs - centre)).astype(jnp.bfloat16)
                dq_parts.append(dot_nn(grad_scores, k_blk))
                dk_part += dot_tn(grad_scores, q_head)
                dv_part += dot_tn(probs.astype(jnp.bfloat16), g_head)
            dk_acc[span, lanes] += dk_part
            dv_acc[span, lanes] += dv_part
            dq = jnp.where(lower, dq_parts[0], dq_parts[1]) * 0.125
            dq = dq * cos_ref[own, lanes] + turn_back(dq * sin_ref[own, lanes])
            dq_ref[rows, lanes] = dq.astype(jnp.bfloat16)
    dk = dk_acc[...]
    dk_ref[...] = (dk * cos_ref[...] + turn_back(dk * sin_ref[...])).astype(jnp.bfloat16)
    dv_ref[...] = dv_acc[...].astype(jnp.bfloat16)


def column_block(rows):
    return pl.BlockSpec((rows, LANES), lambda group: (0, group))


def weight_block(width, which):
    return pl.BlockSpec((1, 1, LANES, width), lambda group: (group, which, 0, 0))


def whole_block(shape):
    return pl.BlockSpec(shape, lambda group: (0,) * len(shape))


def attend(normed_ext, qkv_full, cos_tab, sin_tab, bias):
    ext, width = normed_ext.shape
    count = ext - 2 * HALF
    kind = jnp.bfloat16
    return pl.pallas_call(
        functools.partial(forward_kernel, count // BLOCK),
        grid=(width // LANES,),
        in_specs=[
            whole_block(normed_ext.shape),
            weight_block(width, 0),
            weight_block(width, 1),
            weight_block(width, 2),
            whole_block(cos_tab.shape),
            whole_block(sin_tab.shape),
            whole_block(bias.shape),
        ],
        out_specs=[column_block(count), column_block(ext), column_block(ext), column_block(count)],
        out_shape=[
            jax.ShapeDtypeStruct((count, width), kind),
            jax.ShapeDtypeStruct((ext, width), kind),
            jax.ShapeDtypeStruct((ext, width), kind),
            jax.ShapeDtypeStruct((count, width), kind),
        ],
        compiler_params=pltpu.CompilerParams(vmem_limit_bytes=VMEM_LIMIT),
        cost_estimate=pl.CostEstimate(
            flops=2 * ext * width * 3 * width + 4 * count * 256 * 128 * 16,
            bytes_accessed=2 * (3 * width * width + 5 * ext * width),
            transcendentals=count * 256 * 16,
        ),
        name="attend_forward",
    )(normed_ext, qkv_full, qkv_full, qkv_full, cos_tab, sin_tab, bias)


def attend_back(queries, keys, values, grad_mixture, cos_tab, sin_tab, bias):
    ext, width = keys.shape
    count = ext - 2 * HALF
    kind = jnp.bfloat16
    return pl.pallas_call(
        functools.partial(backward_kernel, count // BLOCK),
        grid=(width // LANES,),
        in_specs=[
            column_block(count),
            column_block(ext),
            column_block(ext),
            column_block(count),
            whole_block(cos_tab.shape),
            whole_block(sin_tab.shape),
            whole_block(bias.shape),
        ],
        out_specs=[column_block(count), column_block(ext), column_block(ext)],
        out_shape=[
            jax.ShapeDtypeStruct((count, width), kind),
            jax.ShapeDtypeStruct((ext, width), kind),
            jax.ShapeDtypeStruct((ext, width), kind),
        ],
        scratch_shapes=[pltpu.VMEM((ext, LANES), jnp.float32), pltpu.VMEM((ext, LANES), jnp.float32)],
        compiler_params=pltpu.CompilerParams(vmem_limit_bytes=VMEM_LIMIT),
        cost_estimate=pl.CostEstimate(
            flops=12 * count * 256 * 128 * 16,
            bytes_accessed=2 * 7 * ext * width,
            transcendentals=count * 256 * 16,
        ),
        name="attend_backward",
    )(queries, keys, values, grad_mixture, cos_tab, sin_tab, bias)


def unit_rows(inputs):
    average = jnp.mean(inputs, 1, keepdims=True)
    centred = inputs - average
    inverse_std = lax.rsqrt(jnp.mean(centred * centred, 1, keepdims=True) + EPS)
    return centred * inverse_std, inverse_std


def norm_backward(grad_normed, unit, inverse_std, gain_vec):
    scaled = grad_normed * gain_vec
    average = jnp.mean(scaled, 1, keepdims=True)
    cross = jnp.mean(scaled * unit, 1, keepdims=True)
    return inverse_std * (scaled - average - unit * cross), jnp.sum(grad_normed * unit, 0)


def swap(array_in, axis):
    return lax.ppermute(array_in, axis, [(0, 1), (1, 0)])


def in_order(mine, other):
    first = lax.axis_index("col") == 0
    return jnp.where(first, mine, other), jnp.where(first, other, mine)


def whole_rows(array_in):
    low_rows, high_rows = jnp.split(array_in, 2, 0)
    mine, theirs = in_order(low_rows, high_rows)
    return jnp.concatenate(in_order(mine, swap(theirs, "col")), 1)


def split_rows(array_in):
    low_cols, high_cols = jnp.split(array_in, 2, 1)
    mine, theirs = in_order(low_cols, high_cols)
    return jnp.concatenate(in_order(mine, swap(theirs, "col")), 0)


def gather_plane(local):
    stack = lax.all_gather(local, CHIPS, axis=0, tiled=False)
    cols = lax.axis_size("col")

    def joined(blocks):
        blocks = blocks.reshape((-1, cols) + local.shape)
        return jnp.concatenate([blocks[:, c] for c in range(cols)], -1)

    return joined(stack), joined(swap(stack, "core"))


def other_core(edge):
    parts = jnp.split(edge, 4, 1)
    return jnp.concatenate([parts[1], parts[0], parts[3], parts[2]], 1)


def core_sum(grad, extra=None):
    mine, theirs = jnp.split(grad, 2, 0)
    if extra is not None:
        mine, theirs = jnp.concatenate([mine, extra], 0), jnp.concatenate([theirs, extra], 0)
    arrived = swap(theirs, "core")
    return (mine.astype(jnp.float32) + arrived.astype(jnp.float32)).astype(jnp.bfloat16)


def chip_stack(parts, feat):
    count = lax.axis_size("x")
    cols = lax.axis_size("col")
    stacked = []
    for x in range(count):
        for c in range(cols):
            lanes = slice(c * feat, (c + 1) * feat)
            pieces = []
            for part, shared in parts:
                block = part.shape[0] if shared else part.shape[0] // count
                start = 0 if shared else x * block
                pieces.append(part[start : start + block, lanes])
            stacked.append(jnp.concatenate(pieces, 0))
    return jnp.stack(stacked)


def scatter(stacked):
    return lax.psum_scatter(stacked, CHIPS, scatter_dimension=0, tiled=False)


def gelu_parts(pre):
    cdf = 0.5 * (1.0 + lax.erf(pre * 0.7071067811865476))
    slope = cdf + pre * jnp.exp(-0.5 * pre * pre) * 0.3989422804014327
    return pre * cdf, slope


def shards(
    tokens,
    segment_ids,
    norm_one,
    qkv_weight,
    attn_out_weight,
    norm_two,
    in_weight,
    out_weight,
    cotangent,
):
    cols = lax.axis_size("col")
    plane = lax.axis_size("x") * lax.axis_size("core") * cols
    place = lax.axis_index(PLANE)
    feat = tokens.shape[1]
    width = feat * cols
    heads_width = qkv_weight.shape[2] * qkv_weight.shape[3]
    hidden = in_weight.shape[2]
    low = jnp.bfloat16

    own_tokens = whole_rows(tokens)
    gains = jnp.stack([norm_one, norm_two])
    gain_one, gain_two = jnp.concatenate(in_order(gains, swap(gains, "col")), 1)
    count = own_tokens.shape[0]
    ahead = [(i, i + 1) for i in range(plane - 1)]
    behind = [(i + 1, i) for i in range(plane - 1)]
    before_rows = lax.ppermute(own_tokens[-HALF:], PLANE, ahead)
    after_rows = lax.ppermute(own_tokens[:HALF], PLANE, behind)
    residual_ext = jnp.concatenate([before_rows, own_tokens, after_rows], 0).astype(jnp.float32)
    unit_ext, inverse_ext = unit_rows(residual_ext)
    normed_ext = (unit_ext * gain_one).astype(low)
    normed_one = normed_ext[HALF:-HALF]

    total = segment_ids.shape[0]
    marks = segment_ids + 16 * (lax.iota(jnp.int32, total) // SEQ)
    marks = jnp.pad(marks, (HALF, HALF), constant_values=-1)
    marks = lax.dynamic_slice_in_dim(marks, place * count, count + 2 * HALF, 0)
    blocks = count // BLOCK
    key_marks = jnp.stack([marks[i * BLOCK : i * BLOCK + BLOCK + WINDOW] for i in range(blocks)])
    query_marks = marks[HALF:-HALF].reshape(blocks, BLOCK)
    shape = (BLOCK, BLOCK + WINDOW)
    distance = lax.broadcasted_iota(jnp.int32, shape, 1) - lax.broadcasted_iota(jnp.int32, shape, 0)
    near = jnp.abs(distance - HALF) <= HALF
    allowed = (query_marks[:, :, None] == key_marks[:, None, :]) & near[None]
    bias = jnp.where(allowed, 0.0, NEG).astype(jnp.float32).reshape(count, BLOCK + WINDOW)

    places = (place * count - HALF + lax.iota(jnp.int32, count + 2 * HALF)) % SEQ
    frequencies = THETA ** (-jnp.arange(32, dtype=jnp.float32) * 2.0 / 64)
    angles = places.astype(jnp.float32)[:, None] * frequencies[None, :]
    cos_tab = jnp.tile(jnp.cos(angles), (1, LANES // 32))
    sin_tab = jnp.tile(jnp.sin(angles), (1, LANES // 32))

    qkv_full = jnp.concatenate(gather_plane(qkv_weight.reshape(feat, 3 * heads_width).T), 0)
    qkv_full = qkv_full.reshape(-1, 3, heads_width, width)
    attn_full = jnp.concatenate(gather_plane(attn_out_weight), 0).reshape(width, width)
    in_blocks = gather_plane(in_weight.transpose(1, 2, 0).reshape(2 * hidden, feat))
    input_full = jnp.concatenate([part[:, :hidden] for part in in_blocks], 0).reshape(-1, width)
    gate_full = jnp.concatenate([part[:, hidden:] for part in in_blocks], 0).reshape(-1, width)
    out_full = jnp.concatenate(gather_plane(out_weight), 0).reshape(-1, width)
    own_cotangent = whole_rows(cotangent)

    queries, keys, values, mixture = attend(normed_ext, qkv_full, cos_tab, sin_tab, bias)
    hidden_rows = own_tokens.astype(jnp.float32) + dot_nn(mixture, attn_full)
    unit_two, inverse_two = unit_rows(hidden_rows)
    normed_two = (unit_two * gain_two).astype(low)
    input_half = dot_nt(normed_two, input_full)
    gate_half = dot_nt(normed_two, gate_full)
    grad_active = dot_nt(own_cotangent, out_full)
    gelu, slope = gelu_parts(input_half)
    active = (gelu * gate_half).astype(low)
    grad_input = (grad_active * gate_half * slope).astype(low)
    grad_gate = (grad_active * gelu).astype(low)
    active, grad_input, grad_gate = lax.optimization_barrier((active, grad_input, grad_gate))

    grad_out = core_sum(dot_tn(active, own_cotangent).astype(low))
    out_part = scatter(chip_stack([(grad_out, False)], feat))
    grad_input_weight = core_sum(dot_tn(grad_input, normed_two).astype(low))
    grad_gate_weight = core_sum(dot_tn(grad_gate, normed_two).astype(low))
    in_stack = chip_stack([(grad_input_weight, False), (grad_gate_weight, False)], feat)
    in_stack, grad_input, grad_gate = lax.optimization_barrier((in_stack, grad_input, grad_gate))
    in_part = scatter(in_stack)
    grad_normed_two = dot_nn(grad_input, input_full) + dot_nn(grad_gate, gate_full)
    branch_two, sum_two = norm_backward(grad_normed_two, unit_two, inverse_two, gain_two)
    grad_hidden = own_cotangent.astype(jnp.float32) + branch_two
    grad_branch = grad_hidden.astype(low)
    result = split_rows((hidden_rows + dot_nn(active, out_full)).astype(low))

    grad_mixture = dot_nt(grad_branch, attn_full).astype(low)
    dq, dk_ext, dv_ext = attend_back(queries, keys, values, grad_mixture, cos_tab, sin_tab, bias)
    edges = jnp.concatenate([dk_ext, dv_ext], 1)
    to_next = lax.ppermute(edges[-HALF:], PLANE, ahead)
    to_prev = lax.ppermute(edges[:HALF], PLANE, behind)
    col = lax.axis_index("col")
    to_next = jnp.where(col == 0, other_core(to_next), to_next)
    to_prev = jnp.where(col == cols - 1, other_core(to_prev), to_prev)
    grad_attn = core_sum(dot_tn(mixture, grad_branch).astype(low))
    middle = edges[HALF:-HALF]
    middle = jnp.concatenate(
        [
            (middle[:HALF].astype(jnp.float32) + to_next.astype(jnp.float32)).astype(low),
            middle[HALF:-HALF],
            (middle[-HALF:].astype(jnp.float32) + to_prev.astype(jnp.float32)).astype(low),
        ],
        0,
    )
    pieces = []
    for start in range(0, width, heads_width):
        for part, first in ((dq, 0), (middle, 0), (middle, width)):
            pieces.append(part[:, first + start : first + start + heads_width])
    grad_joined = lax.optimization_barrier(jnp.concatenate(pieces, 1))
    grad_normed_one = dot_nn(grad_joined, qkv_full.reshape(-1, width))
    branch_one, sum_one = norm_backward(
        grad_normed_one, unit_ext[HALF:-HALF], inverse_ext[HALF:-HALF], gain_one
    )
    grad_tokens = split_rows((grad_hidden + branch_one).astype(low)).astype(jnp.float32)

    sums = jnp.pad(jnp.stack([sum_one, sum_two]).astype(low), ((0, 14), (0, 0)))
    grad_qkv = core_sum(dot_tn(grad_joined, normed_one).astype(low), sums)
    heads_rows = grad_qkv.shape[0] - 16
    late_stack = chip_stack(
        [(grad_qkv[:heads_rows], False), (grad_qkv[heads_rows:], True), (grad_attn, False)], feat
    )
    out_sum, in_sum = lax.psum((out_part, in_part), "dp")
    late_stack, out_sum, in_sum = lax.optimization_barrier((late_stack, out_sum, in_sum))
    late_sum = lax.psum(scatter(late_stack), "dp").astype(jnp.float32)
    qkv_rows = 3 * heads_width
    return (
        result,
        grad_tokens,
        late_sum[qkv_rows],
        late_sum[:qkv_rows].T.reshape(qkv_weight.shape),
        late_sum[qkv_rows + 16 :],
        late_sum[qkv_rows + 1],
        in_sum.astype(jnp.float32).reshape(2, hidden, feat).transpose(2, 0, 1),
        out_sum.astype(jnp.float32),
    )


def solution(mesh):
    dp, row, col = (mesh.shape[name] for name in ("dp", "row", "col"))
    devices = mesh.devices.reshape(dp, row // 2, 2, col)
    fine = jax.sharding.Mesh(devices, ("dp", "x", "core", "col"))
    row = ("x", "core")
    rows = ("dp", "x", "core")
    return jax.shard_map(
        shards,
        mesh=fine,
        in_specs=(
            P(rows, "col"),
            P("dp"),
            P("col"),
            P("col", None, row, None),
            P(row, "col"),
            P("col"),
            P("col", None, row),
            P(row, "col"),
            P(rows, "col"),
        ),
        out_specs=(
            P(rows, "col"),
            P(rows, "col"),
            P("col"),
            P("col", None, row, None),
            P(row, "col"),
            P("col"),
            P("col", None, row),
            P(row, "col"),
        ),
        check_vma=False,
    )
```
